512 devices in a mesh: row: 32 (over z, y_hi, core), col: 16 (over x, y_lo).
Axes of the slice: x: 4, y: 8 (y_hi: 2, y_lo: 4; y = y_hi * 4 + y_lo), z: 8, core: 2. Of those that a mesh axis runs over, the one named last changes fastest.
Arguments:
- query_state: float32 [65536, 256], P(('row', 'col')), may hold values from 0 to 2
- doc_state: float32 [16384, 256], P(('col', 'row')), may hold values from 0 to 2
- query_degree: int32 [65536], P(('row', 'col')), may hold values from 385 to 6144
- doc_degree: int32 [16384], P(('col', 'row')), may hold values from 1537 to 24576
- tile_slots: int32 [32, 16, 96], P('row', 'col'), may hold values from 0 to 127, as said below
- tile_count: int32 [32, 16], P('row', 'col'), may hold values from 16 to 96, as said below
- tile_bits: int32 [32, 16, 96, 128, 16], P('row', 'col'), may hold values from 0 to 255
- query_self_w: float32 [256, 256], replicated, may hold values from -0.375 to 0.375
- query_nbr_w: float32 [256, 256], replicated, may hold values from -0.375 to 0.375
- query_bias: float32 [256], replicated, may hold values from -0.5 to 0.5
- doc_self_w: float32 [256, 256], replicated, may hold values from -0.375 to 0.375
- doc_nbr_w: float32 [256, 256], replicated, may hold values from -0.375 to 0.375
- doc_bias: float32 [256], replicated, may hold values from -0.5 to 0.5
Outputs:
- query_out: float32 [65536, 256], P(('row', 'col'))
- doc_out: float32 [16384, 256], P(('col', 'row'))
The draws below stay inside these ranges and needn't reach their ends.
Inputs may be any that keep to these rules, and one draw needn't show every extreme that they name: `tile_slots`: entries 0 to tile_count - 1 of a device's list are distinct and rising; slot s stands for its local query block s // 8 and local document block s % 8; the entries after them are other slots and stand for no tile. `tile_count`: some device holds 96 live tiles in every draw.
All inputs are finite; a program needn't handle non-finite values.
Results may differ from the reference program's by a relative error of at most 0.0003.
Values sent between devices are 32-bit elements; how exact they have to be, the bound alone decides.
A program may use at most 64 MiB of HBM per device.

```python
import jax
import jax.numpy as jnp
from jax import lax

F = 256
QT = 16
DT = 8
TMAX = 96
QN = 65536
DN = 16384
N_ROW = 32
N_COL = 16


def tile_layout(key):
    count_key = jax.random.fold_in(key, 11)
    order_key = jax.random.fold_in(key, 12)
    full_key = jax.random.fold_in(key, 13)
    device_total = N_ROW * N_COL
    lowest = max(1, TMAX // 6)
    counts = jax.random.randint(count_key, (device_total,), lowest, TMAX // 2 + 1)
    busiest = jax.random.randint(full_key, (), 0, device_total)
    counts = jnp.where(jnp.arange(device_total) == busiest, TMAX, counts).astype(jnp.int32)
    slot_total = QT * DT
    scores = jax.random.randint(order_key, (device_total, slot_total), 0, 1 << 20) * slot_total + jnp.arange(slot_total)[None, :]
    chosen = jnp.argsort(scores, axis=1)[:, :TMAX].astype(jnp.int32)
    ranked = jnp.where(jnp.arange(TMAX)[None, :] < counts[:, None], chosen, chosen + slot_total)
    ordered = (jnp.sort(ranked, axis=1) % slot_total).astype(jnp.int32)
    return (ordered.reshape(N_ROW, N_COL, TMAX), counts.reshape(N_ROW, N_COL))


def draw_tile_slots(key, part):
    slot_ids, live_count = tile_layout(key)
    return slot_ids


def draw_tile_count(key, part):
    slot_ids, live_count = tile_layout(key)
    return live_count


def with_ends(array, rng, low, high):
    dims = array.shape
    place = [jax.random.randint(jax.random.fold_in(rng, axis), (), 0, dims[axis]) for axis in range(len(dims))]
    array = array.at[tuple(place)].set(low)
    longest = dims.index(max(dims))
    place[longest] = (place[longest] + 1) % dims[longest]
    return array.at[tuple(place)].set(high)


def block_levels(own_key, extent, cuts, least, top_value):
    def one(position, blocks):
        steps = jax.random.uniform(jax.random.fold_in(jax.random.fold_in(own_key, 6), position), (blocks,), jnp.float32, least / len(cuts), top_value / len(cuts))
        return jnp.repeat(jnp.exp(steps), extent[position] // blocks).reshape((-1,) + (1,) * (len(extent) - position - 1))

    factor_of = one(*cuts[0])
    for cut in cuts[1:]:
        factor_of = factor_of * one(*cut)
    return factor_of


def bell_draw(rng, extent, width, limit, kind=jnp.bfloat16):
    drawn = width * jax.random.normal(rng, extent, jnp.float32)
    return jnp.clip(drawn, min=-limit, max=limit).astype(kind)


def setup_inputs(seed: int = 0) -> dict:
    key_of = jax.random.split(jax.random.key(seed), 14)
    return {
        "query_state": jnp.clip(2.0 * jax.random.uniform(key_of[0], (QN, F), jnp.float32) ** block_levels(key_of[0], (QN, F), ((0, 512),), -0.2, 0.2), 0.0, 2.0),
        "doc_state": jnp.clip(2.0 * jax.random.uniform(key_of[1], (DN, F), jnp.float32) ** block_levels(key_of[1], (DN, F), ((0, 512),), -0.2, 0.2), 0.0, 2.0),
        "query_degree": with_ends(jax.random.randint(key_of[2], (QN,), 64 * TMAX // QT + 1, 1024 * TMAX // QT + 1), jax.random.fold_in(key_of[2], 1), 64 * TMAX // QT + 1, (1024 * TMAX // QT + 1) - 1).astype(jnp.int32),
        "doc_degree": with_ends(jax.random.randint(key_of[3], (DN,), 128 * TMAX // DT + 1, 2048 * TMAX // DT + 1), jax.random.fold_in(key_of[3], 1), 128 * TMAX // DT + 1, (2048 * TMAX // DT + 1) - 1).astype(jnp.int32),
        "tile_slots": draw_tile_slots(jax.random.fold_in(key_of[13], 71), 0),
        "tile_count": draw_tile_count(jax.random.fold_in(key_of[13], 71), 0),
        "tile_bits": with_ends(jax.random.randint(key_of[6], (N_ROW, N_COL, TMAX, 128, 16), 0, 256), jax.random.fold_in(key_of[6], 1), 0, 255).astype(jnp.int32),
        "query_self_w": bell_draw(key_of[7], (F, F), F ** -0.5, 0.375, jnp.float32),
        "query_nbr_w": bell_draw(key_of[8], (F, F), F ** -0.5, 0.375, jnp.float32),
        "query_bias": jnp.clip(jax.random.uniform(key_of[9], (F,), jnp.float32, -0.5, 0.5), -0.5, 0.5),
        "doc_self_w": bell_draw(key_of[10], (F, F), F ** -0.5, 0.375, jnp.float32),
        "doc_nbr_w": bell_draw(key_of[11], (F, F), F ** -0.5, 0.375, jnp.float32),
        "doc_bias": jnp.clip(jax.random.uniform(key_of[12], (F,), jnp.float32, -0.5, 0.5), -0.5, 0.5),
    }


HIGHEST = lax.Precision.HIGHEST

def unpack(packed):
    columns = jnp.arange(128, dtype=jnp.int32)
    spread = jnp.repeat(packed, 8, axis=-1)
    return jnp.bitwise_and(jnp.right_shift(spread, columns % 8), 1).astype(jnp.float32)

def dense_layer(state_in, neighbours, self_weight, neighbour_weight, bias_row):
    before = jnp.dot(state_in, self_weight, precision=HIGHEST, preferred_element_type=jnp.float32)
    before = before + jnp.dot(neighbours, neighbour_weight, precision=HIGHEST, preferred_element_type=jnp.float32) + bias_row
    hidden = jnp.maximum(before, 0.0)
    return hidden * lax.rsqrt(lax.optimization_barrier(jnp.mean(hidden * hidden, axis=-1, keepdims=True)) + 1e-05)

def tile_lists(tile_slots, tile_count, tile_bits):
    device_total = N_ROW * N_COL
    device_ids = jnp.arange(device_total, dtype=jnp.int32)
    slot_ids = tile_slots.reshape(device_total, TMAX).astype(jnp.int32)
    live_slots = jnp.arange(TMAX, dtype=jnp.int32)[None, :] < tile_count.reshape(device_total, 1)
    query_blocks = (device_ids // N_COL)[:, None] * QT + slot_ids // DT
    doc_blocks = (device_ids % N_COL)[:, None] * DT + slot_ids % DT
    packed = tile_bits.reshape(device_total, TMAX, 128, 16)
    return (query_blocks.astype(jnp.int32), doc_blocks.astype(jnp.int32), live_slots, packed)

def forward_sum(sources, query_blocks, doc_blocks, live_slots, packed):

    def visit(running, inputs):
        query_ids, doc_ids, alive_now, words_in = inputs
        tile_mask = unpack(words_in) * alive_now.astype(jnp.float32)[:, None, None]
        product = jnp.einsum('tqd,tdf->tqf', tile_mask, sources[doc_ids], precision=HIGHEST)
        return (running.at[query_ids].add(product), None)
    begin_with = jnp.zeros((N_ROW * QT, 128, F), jnp.float32)
    running, unused = lax.scan(visit, begin_with, (query_blocks, doc_blocks, live_slots, packed))
    return running

def backward_sum(sources, query_blocks, doc_blocks, live_slots, packed):

    def visit(running, inputs):
        query_ids, doc_ids, alive_now, words_in = inputs
        tile_mask = unpack(words_in) * alive_now.astype(jnp.float32)[:, None, None]
        product = jnp.einsum('tqd,tqf->tdf', tile_mask, sources[query_ids], precision=HIGHEST)
        return (running.at[doc_ids].add(product), None)
    begin_with = jnp.zeros((N_COL * DT, 128, F), jnp.float32)
    running, unused = lax.scan(visit, begin_with, (query_blocks, doc_blocks, live_slots, packed))
    return running

def reference(query_state, doc_state, query_degree, doc_degree, tile_slots, tile_count, tile_bits, query_self_w, query_nbr_w, query_bias, doc_self_w, doc_nbr_w, doc_bias):
    query_blocks, doc_blocks, live_slots, packed = tile_lists(tile_slots, tile_count, tile_bits)
    query_inverse = lax.rsqrt(query_degree.astype(jnp.float32))[:, None]
    doc_inverse = lax.rsqrt(doc_degree.astype(jnp.float32))[:, None]
    doc_scaled = (doc_state * doc_inverse).reshape(N_COL * DT, 128, F)
    query_agg = forward_sum(doc_scaled, query_blocks, doc_blocks, live_slots, packed).reshape(QN, F) * query_inverse
    query_out = dense_layer(query_state, query_agg, query_self_w, query_nbr_w, query_bias)
    query_scaled = (query_out * query_inverse).reshape(N_ROW * QT, 128, F)
    doc_agg = backward_sum(query_scaled, query_blocks, doc_blocks, live_slots, packed).reshape(DN, F) * doc_inverse
    doc_out = dense_layer(doc_state, doc_agg, doc_self_w, doc_nbr_w, doc_bias)
    return (query_out, doc_out)
```

```python
import functools

import jax
import jax.numpy as jnp
from jax import lax
from jax.experimental import pallas as pl
from jax.experimental.pallas import tpu as pltpu
from jax.sharding import PartitionSpec as P

QT = 16
DT = 8
TMAX = 96
NX, NYL, NZ, NYH = 4, 4, 8, 2
MESH = pl.DeviceIdType.MESH
HIGHEST = lax.Precision.HIGHEST


def split_two(x):
    high = x.astype(jnp.bfloat16)
    low = (x - high.astype(jnp.float32)).astype(jnp.bfloat16)
    return high, low


def column_of(row_vector):
    n = row_vector.shape[1]
    i = lax.broadcasted_iota(jnp.int32, (n, n), 0)
    j = lax.broadcasted_iota(jnp.int32, (n, n), 1)
    return jnp.sum(jnp.where(i == j, row_vector, 0.0), axis=1, keepdims=True)


def rms(before):
    hidden = jnp.maximum(before, 0.0)
    return hidden * lax.rsqrt(jnp.mean(hidden * hidden, axis=-1, keepdims=True) + 1e-05)


def dot_full(a, b):
    return jnp.dot(a, b, precision=HIGHEST, preferred_element_type=jnp.float32)


def kernel(
    qs_ref, ds_ref, qdeg_ref, ddeg_ref, slots_ref, count_ref, bits_ref,
    qw_ref, qnw_ref, qb_ref, dw_ref, dnw_ref, db_ref,
    qo_ref, do_ref,
    at, dg, lhs, part, r2, rx, sx, ry, qg, wq, yd, rc, zd, rd, qself, dself,
    s1, v1, s1c, v1c, sx1, vx1, sx2, vx2, sy, vy, s3, v3, s4c, v4c, s4, v4,
):
    row = lax.axis_index("row")
    col = lax.axis_index("col")
    z0, h0, c0 = row // 4, (row // 2) % 2, row % 2
    x0, y0 = col // NYL, col % NYL
    m0 = z0 * 2 + h0
    sibling = (row + 1 - 2 * c0, col)

    def mate(k):
        dz, dh = k // 2, k % 2
        return (z0 + dz) % NZ * 2 + (h0 + dh) % 2

    def mate_from(k):
        dz, dh = k // 2, k % 2
        return (z0 + NZ - dz) % NZ * 2 + (h0 + dh) % 2

    def x_dev(dx):
        return (row, (x0 + dx + NX) % NX * NYL + y0)

    def y_dev(k):
        return (row, x0 * NYL + (y0 + k) % NYL)

    def send(src, dst, ssem, rsem, dev):
        copy = pltpu.make_async_remote_copy(
            src_ref=src, dst_ref=dst, send_sem=ssem, recv_sem=rsem, device_id=dev, device_id_type=MESH
        )
        copy.start()
        return copy

    def sent(src, dst, ssem, rsem):
        pltpu.make_async_remote_copy(
            src_ref=src, dst_ref=dst, send_sem=ssem, recv_sem=rsem, device_id=sibling, device_id_type=MESH
        ).wait_send()

    def got(src, dst, ssem, rsem):
        pltpu.make_async_remote_copy(
            src_ref=src, dst_ref=dst, send_sem=ssem, recv_sem=rsem, device_id=sibling, device_id_type=MESH
        ).wait_recv()

    barrier = pltpu.get_barrier_semaphore()

    def greet(dev):
        pl.semaphore_signal(barrier, inc=1, device_id=dev, device_id_type=MESH)

    greet(sibling)
    greet(x_dev(1))
    greet(x_dev(-1))
    for k in range(1, NYL):
        greet(y_dev(k))

    def greet_mate(k, _):
        greet((mate(k) * 2 + c0, col))
        return 0

    lax.fori_loop(1, NZ * NYH, greet_mate, 0)

    dinv = column_of(lax.rsqrt(ddeg_ref[...].astype(jnp.float32)))
    qinv_row = lax.rsqrt(qdeg_ref[...].astype(jnp.float32))
    qinv = column_of(qinv_row)
    scaled = ds_ref[...] * dinv
    for h in range(2):
        dg[h, row] = scaled[:, h * 128 : (h + 1) * 128]

    pl.semaphore_wait(barrier, 1 + 2 + NYL - 1 + NZ * NYH - 1)

    for h in range(2):
        send(dg.at[h, row], dg.at[h, row], s1c.at[h, 0], v1c.at[h, 0], sibling)

        def push(k, _, h=h):
            send(dg.at[h, row], dg.at[h, row], s1.at[h, k], v1.at[h, k], (mate(k) * 2 + c0, col))
            return 0

        lax.fori_loop(1, NZ * NYH, push, 0)

    shifts = lax.broadcasted_iota(jnp.int32, (8, 128), 0)
    count = count_ref[0, 0]

    def unpack(s, t):
        t_in = jnp.minimum(t, TMAX - 1)
        hit = jnp.logical_and(t < count, slots_ref[0, t_in] == s)
        keep = jnp.where(hit, 1, 0)
        words = bits_ref[t_in] * keep
        rows = []
        for w in range(16):
            spread = jnp.broadcast_to(words[w : w + 1, :], (8, 128))
            rows.append(jnp.bitwise_and(jnp.right_shift(spread, shifts), 1).astype(jnp.float32))
        tile = jnp.concatenate(rows, axis=0).astype(jnp.bfloat16)
        return tile, t + keep

    def unpack_pair(p, t):
        for half in range(2):
            for d in range(DT):
                tile, t = unpack((2 * p + half) * DT + d, t)
                at[p, d * 128 : (d + 1) * 128, half * 128 : (half + 1) * 128] = tile
        return t

    lax.fori_loop(0, QT // 2, unpack_pair, jnp.int32(0))

    qself[...] = dot_full(qs_ref[...], qw_ref[...]) + qb_ref[...]
    dself[...] = dot_full(ds_ref[...], dw_ref[...]) + db_ref[...]

    def forward_docs(h):
        def pass_on(k, _):
            r = mate_from(k) * 2 + c0
            got(dg.at[h, r], dg.at[h, r], s1.at[h, k], v1.at[h, k])
            send(dg.at[h, r], dg.at[h, r], s1c.at[h, k], v1c.at[h, k], sibling)
            return 0

        lax.fori_loop(1, NZ * NYH, pass_on, 0)

    def wait_docs(h):
        def one(k, _):
            r = mate_from(k) * 2 + 1 - c0
            got(dg.at[h, r], dg.at[h, r], s1c.at[h, k], v1c.at[h, k])
            return 0

        lax.fori_loop(0, NZ * NYH, one, 0)

    def multiply(h, x):
        for j in range(2):
            both = jnp.dot(lhs[...], at[2 * x + j], preferred_element_type=jnp.float32)
            whole = both[:128] + both[128:]
            part[h, 4 * x + 2 * j] = whole[:, :128]
            part[h, 4 * x + 2 * j + 1] = whole[:, 128:]

    xp, xm, xo = (x0 + 1) % NX, (x0 + NX - 1) % NX, (x0 + 2) % NX

    def start_x(h):
        docs = dg[h].reshape(DT * 128, 128).T
        high, low = split_two(docs)
        lhs[0:128, :] = high
        lhs[128:256, :] = low
        multiply(h, xo)
        send(part.at[h, pl.ds(4 * xo, 2)], r2.at[h, 0], sx1.at[h, 0], vx1.at[h, 0], x_dev(1))
        send(part.at[h, pl.ds(4 * xo + 2, 2)], r2.at[h, 1], sx1.at[h, 1], vx1.at[h, 1], x_dev(-1))
        multiply(h, xp)
        send(part.at[h, pl.ds(4 * xp + 2, 2)], rx.at[h, 0, 1], sx2.at[h, 0], vx2.at[h, 0], x_dev(1))
        multiply(h, xm)
        send(part.at[h, pl.ds(4 * xm, 2)], rx.at[h, 1, 0], sx2.at[h, 1], vx2.at[h, 1], x_dev(-1))
        multiply(h, x0)

    def second_x(h):
        got(r2.at[h, 0], r2.at[h, 0], sx1.at[h, 0], vx1.at[h, 0])
        part[h, pl.ds(4 * xp, 2)] += r2[h, 0]
        send(part.at[h, pl.ds(4 * xp, 2)], rx.at[h, 0, 0], sx2.at[h, 2], vx2.at[h, 2], x_dev(1))
        got(r2.at[h, 1], r2.at[h, 1], sx1.at[h, 1], vx1.at[h, 1])
        part[h, pl.ds(4 * xm + 2, 2)] += r2[h, 1]
        send(part.at[h, pl.ds(4 * xm + 2, 2)], rx.at[h, 1, 1], sx2.at[h, 3], vx2.at[h, 3], x_dev(-1))

    def start_y(h):
        for i, (a, b) in enumerate(((0, 1), (1, 0), (0, 0), (1, 1))):
            got(rx.at[h, a, b], rx.at[h, a, b], sx2.at[h, i], vx2.at[h, i])
        for b in range(2):
            sx[h, 2 * b : 2 * b + 2] = part[h, pl.ds(4 * x0 + 2 * b, 2)] + rx[h, 0, b] + rx[h, 1, b]
        for k in range(1, NYL):
            send(sx.at[h, (y0 + k) % NYL], ry.at[h, k - 1], sy.at[h, k - 1], vy.at[h, k - 1], y_dev(k))

    def end_y(h):
        for k in range(NYL - 1):
            got(ry.at[h, k], ry.at[h, k], sy.at[h, k], vy.at[h, k])
        return ((sx[h, y0] + ry[h, 0]) + (ry[h, 1] + ry[h, 2])) * qinv_row

    forward_docs(0)
    forward_docs(1)
    wait_docs(0)
    start_x(0)
    wait_docs(1)
    start_x(1)
    second_x(0)
    second_x(1)
    start_y(0)
    start_y(1)
    agg = jnp.concatenate([end_y(0).T, end_y(1).T], axis=1)

    query_out = rms(qself[...] + dot_full(agg, qnw_ref[...]))
    qo_ref[...] = query_out
    query_scaled = query_out * qinv
    for h in range(2):
        qg[h, col] = query_scaled[:, h * 128 : (h + 1) * 128]

    def share(h, block, sem, dev):
        send(qg.at[h, block], qg.at[h, block], s3.at[h, sem], v3.at[h, block], dev)

    def have(h, block):
        got(qg.at[h, block], qg.at[h, block], s3.at[h, 0], v3.at[h, block])

    def own_out(h):
        for k in range(1, NYL):
            share(h, col, k - 1, y_dev(k))
        share(h, col, 3, x_dev(1))
        share(h, col, 4, x_dev(-1))

    def y_on(h):
        for k in range(1, NYL):
            block = x0 * NYL + (y0 + NYL - k) % NYL
            have(h, block)
            share(h, block, 3 + 2 * k, x_dev(1))
            share(h, block, 4 + 2 * k, x_dev(-1))

    def x_on(h, k):
        y = (y0 + NYL - k) % NYL
        way = 1 - 2 * (y // 2)
        block = (x0 - way + NX) % NX * NYL + y
        have(h, block)
        share(h, block, 11 + k, x_dev(way))

    def x_rest(h):
        for k in range(NYL):
            y = (y0 + NYL - k) % NYL
            way = 1 - 2 * (y // 2)
            have(h, (x0 + way + NX) % NX * NYL + y)
        for y in range(NYL):
            have(h, xo * NYL + y)

    own_out(0)
    own_out(1)
    y_on(0)
    x_on(0, 0)
    y_on(1)
    for k in range(1, NYL):
        x_on(0, k)
    x_on(1, 0)
    x_rest(0)

    def back(h):
        for j in range(QT // 2):
            high, low = split_two(qg[h, 2 * j : 2 * j + 2].reshape(256, 128))
            wq[j, :, 0:128] = high
            wq[j, :, 128:256] = low

        def rows_of(i, _):
            total = jnp.zeros((256, 256), jnp.float32)
            for j in range(QT // 2):
                total += jnp.dot(at[j, pl.ds(i * 256, 256), :], wq[j], preferred_element_type=jnp.float32)
            whole = (total[:, :128] + total[:, 128:]).reshape(4, 2, 32, 128)
            yd[h, 0, pl.ds(i * 4, 4)] = whole[:, 0]
            yd[h, 1, pl.ds(i * 4, 4)] = whole[:, 1]
            return 0

        lax.fori_loop(0, 4, rows_of, 0)
        send(yd.at[h, 1 - c0], rc.at[h], s4c.at[h], v4c.at[h], sibling)

    def spread(h):
        got(rc.at[h], rc.at[h], s4c.at[h], v4c.at[h])
        zd[h] = yd[h, c0] + rc[h]

        def push(k, _):
            send(zd.at[h, mate(k)], rd.at[h, k], s4.at[h, k], v4.at[h, k], (mate(k) * 2 + c0, col))
            return 0

        lax.fori_loop(1, NZ * NYH, push, 0)

    def collect(h):
        def one(k, total):
            got(rd.at[h, k], rd.at[h, k], s4.at[h, k], v4.at[h, k])
            return total + rd[h, k]

        return lax.fori_loop(1, NZ * NYH, one, zd[h, m0])

    back(0)
    for k in range(1, NYL):
        x_on(1, k)
    spread(0)
    x_rest(1)
    back(1)
    spread(1)
    doc_agg = jnp.concatenate([collect(0), collect(1)], axis=1) * dinv
    do_ref[...] = rms(dself[...] + dot_full(doc_agg, dnw_ref[...]))

    for h in range(2):
        def out_docs(k, _, h=h):
            sent(dg.at[h, row], dg.at[h, row], s1.at[h, k], v1.at[h, k])
            sent(zd.at[h, 0], rd.at[h, k], s4.at[h, k], v4.at[h, k])
            return 0

        lax.fori_loop(1, NZ * NYH, out_docs, 0)

        def out_sibling(k, _, h=h):
            sent(dg.at[h, row], dg.at[h, row], s1c.at[h, k], v1c.at[h, k])
            return 0

        lax.fori_loop(0, NZ * NYH, out_sibling, 0)
        for i in range(2):
            sent(r2.at[h, i], r2.at[h, i], sx1.at[h, i], vx1.at[h, i])
        for i in range(4):
            sent(rx.at[h, 0, 0], rx.at[h, 0, 0], sx2.at[h, i], vx2.at[h, i])
        for k in range(NYL - 1):
            sent(ry.at[h, k], ry.at[h, k], sy.at[h, k], vy.at[h, k])

        def out_query(k, _, h=h):
            sent(qg.at[h, 0], qg.at[h, 0], s3.at[h, k], v3.at[h, 0])
            return 0

        lax.fori_loop(0, 15, out_query, 0)
        sent(rc.at[h], rc.at[h], s4c.at[h], v4c.at[h])


def local(
    query_state, doc_state, query_degree, doc_degree, tile_slots, tile_count, tile_bits,
    query_self_w, query_nbr_w, query_bias, doc_self_w, doc_nbr_w, doc_bias,
):
    f32, bf16 = jnp.float32, jnp.bfloat16
    vmem = pl.BlockSpec(memory_space=pltpu.VMEM)
    smem = pl.BlockSpec(memory_space=pltpu.SMEM)
    dma = pltpu.SemaphoreType.DMA
    bits = jnp.swapaxes(tile_bits[0, 0], 1, 2)
    return pl.pallas_call(
        kernel,
        out_shape=(
            jax.ShapeDtypeStruct((128, 256), f32),
            jax.ShapeDtypeStruct((32, 256), f32),
        ),
        in_specs=[vmem, vmem, vmem, vmem, smem, smem] + [vmem] * 7,
        out_specs=(vmem, vmem),
        scratch_shapes=[
            pltpu.VMEM((QT // 2, DT * 128, 256), bf16),
            pltpu.VMEM((2, 32, 32, 128), f32),
            pltpu.VMEM((256, DT * 128), bf16),
            pltpu.VMEM((2, QT, 128, 128), f32),
            pltpu.VMEM((2, 2, 2, 128, 128), f32),
            pltpu.VMEM((2, 2, 2, 2, 128, 128), f32),
            pltpu.VMEM((2, NYL, 128, 128), f32),
            pltpu.VMEM((2, NYL - 1, 128, 128), f32),
            pltpu.VMEM((2, QT, 128, 128), f32),
            pltpu.VMEM((QT // 2, 256, 256), bf16),
            pltpu.VMEM((2, 2, 16, 32, 128), f32),
            pltpu.VMEM((2, 16, 32, 128), f32),
            pltpu.VMEM((2, 16, 32, 128), f32),
            pltpu.VMEM((2, 16, 32, 128), f32),
            pltpu.VMEM((128, 256), f32),
            pltpu.VMEM((32, 256), f32),
            dma((2, 16)), dma((2, 16)), dma((2, 16)), dma((2, 16)),
            dma((2, 2)), dma((2, 2)), dma((2, 4)), dma((2, 4)),
            dma((2, 3)), dma((2, 3)), dma((2, 15)), dma((2, 16)),
            dma((2,)), dma((2,)), dma((2, 16)), dma((2, 16)),
        ],
        compiler_params=pltpu.CompilerParams(
            collective_id=0, has_side_effects=True, vmem_limit_bytes=40 << 20
        ),
    )(
        query_state, doc_state, query_degree.reshape(1, 128), doc_degree.reshape(1, 32),
        tile_slots[0], tile_count, bits,
        query_self_w, query_nbr_w, query_bias.reshape(1, 256),
        doc_self_w, doc_nbr_w, doc_bias.reshape(1, 256),
    )


def solution(mesh):
    placed = (
        P(("row", "col"), None),
        P(("col", "row"), None),
        P(("row", "col")),
        P(("col", "row")),
        P("row", "col", None),
        P("row", "col"),
        P("row", "col", None, None, None),
        P(),
        P(),
        P(),
        P(),
        P(),
        P(),
    )
    return jax.shard_map(
        local,
        mesh=mesh,
        in_specs=placed,
        out_specs=(P(("row", "col"), None), P(("col", "row"), None)),
        check_vma=False,
    )
```

```python
import functools

import jax
import jax.numpy as jnp
from jax import lax
from jax.experimental import pallas as pl
from jax.experimental.pallas import tpu as pltpu
from jax.sharding import PartitionSpec as P

QT = 16
DT = 8
TMAX = 96
NX, NYL, NZ, NYH = 4, 4, 8, 2
MESH = pl.DeviceIdType.MESH
HIGHEST = lax.Precision.HIGHEST


def split_two(x):
    high = x.astype(jnp.bfloat16)
    low = (x - high.astype(jnp.float32)).astype(jnp.bfloat16)
    return high, low


def column_of(row_vector):
    n = row_vector.shape[1]
    i = lax.broadcasted_iota(jnp.int32, (n, n), 0)
    j = lax.broadcasted_iota(jnp.int32, (n, n), 1)
    return jnp.sum(jnp.where(i == j, row_vector, 0.0), axis=1, keepdims=True)


def rms(before):
    hidden = jnp.maximum(before, 0.0)
    return hidden * lax.rsqrt(jnp.mean(hidden * hidden, axis=-1, keepdims=True) + 1e-05)


def dot_full(a, b):
    return jnp.dot(a, b, precision=HIGHEST, preferred_element_type=jnp.float32)


def kernel(
    qs_ref, ds_ref, qdeg_ref, ddeg_ref, slots_ref, count_ref, bits_ref,
    qw_ref, qnw_ref, qb_ref, dw_ref, dnw_ref, db_ref,
    qo_ref, do_ref,
    at, dg, lhs, part, r2, rx, sx, ry, qg, wq, yd, rc, zd, rd, qself, dself,
    s1, v1, s1c, v1c, sx1, vx1, sx2, vx2, sy, vy, s3, v3, s4c, v4c, s4, v4,
):
    row = lax.axis_index("row")
    col = lax.axis_index("col")
    z0, h0, c0 = row // 4, (row // 2) % 2, row % 2
    x0, y0 = col // NYL, col % NYL
    m0 = z0 * 2 + h0
    sibling = (row + 1 - 2 * c0, col)

    def mate(k):
        dz, dh = k // 2, k % 2
        return (z0 + dz) % NZ * 2 + (h0 + dh) % 2

    def mate_from(k):
        dz, dh = k // 2, k % 2
        return (z0 + NZ - dz) % NZ * 2 + (h0 + dh) % 2

    def x_dev(dx):
        return (row, (x0 + dx + NX) % NX * NYL + y0)

    def y_dev(k):
        return (row, x0 * NYL + (y0 + k) % NYL)

    def send(src, dst, ssem, rsem, dev):
        copy = pltpu.make_async_remote_copy(
            src_ref=src, dst_ref=dst, send_sem=ssem, recv_sem=rsem, device_id=dev, device_id_type=MESH
        )
        copy.start()
        return copy

    def sent(src, dst, ssem, rsem):
        pltpu.make_async_remote_copy(
            src_ref=src, dst_ref=dst, send_sem=ssem, recv_sem=rsem, device_id=sibling, device_id_type=MESH
        ).wait_send()

    def got(src, dst, ssem, rsem):
        pltpu.make_async_remote_copy(
            src_ref=src, dst_ref=dst, send_sem=ssem, recv_sem=rsem, device_id=sibling, device_id_type=MESH
        ).wait_recv()

    barrier = pltpu.get_barrier_semaphore()

    def greet(dev):
        pl.semaphore_signal(barrier, inc=1, device_id=dev, device_id_type=MESH)

    greet(sibling)
    greet(x_dev(1))
    greet(x_dev(-1))
    for k in range(1, NYL):
        greet(y_dev(k))

    def greet_mate(k, _):
        greet((mate(k) * 2 + c0, col))
        return 0

    lax.fori_loop(1, NZ * NYH, greet_mate, 0)

    dinv = column_of(lax.rsqrt(ddeg_ref[...].astype(jnp.float32)))
    qinv_row = lax.rsqrt(qdeg_ref[...].astype(jnp.float32))
    qinv = column_of(qinv_row)
    scaled = ds_ref[...] * dinv
    for h in range(2):
        dg[h, row] = scaled[:, h * 128 : (h + 1) * 128]

    pl.semaphore_wait(barrier, 1 + 2 + NYL - 1 + NZ * NYH - 1)

    for h in range(2):
        send(dg.at[h, row], dg.at[h, row], s1c.at[h, 0], v1c.at[h, 0], sibling)

        def push(k, _, h=h):
            send(dg.at[h, row], dg.at[h, row], s1.at[h, k], v1.at[h, k], (mate(k) * 2 + c0, col))
            return 0

        lax.fori_loop(1, NZ * NYH, push, 0)

    shifts = lax.broadcasted_iota(jnp.int32, (8, 128), 0)
    count = count_ref[0, 0]

    def unpack(s, t):
        t_in = jnp.minimum(t, TMAX - 1)
        hit = jnp.logical_and(t < count, slots_ref[0, t_in] == s)
        keep = jnp.where(hit, 1, 0)
        words = bits_ref[t_in] * keep
        rows = []
        for w in range(16):
            spread = jnp.broadcast_to(words[w : w + 1, :], (8, 128))
            rows.append(jnp.bitwise_and(jnp.right_shift(spread, shifts), 1).astype(jnp.float32))
        tile = jnp.concatenate(rows, axis=0).astype(jnp.bfloat16)
        return tile, t + keep

    def unpack_pair(p, t):
        for half in range(2):
            for d in range(DT):
                tile, t = unpack((2 * p + half) * DT + d, t)
                at[p, d * 128 : (d + 1) * 128, half * 128 : (half + 1) * 128] = tile
        return t

    lax.fori_loop(0, QT // 2, unpack_pair, jnp.int32(0))

    qself[...] = dot_full(qs_ref[...], qw_ref[...]) + qb_ref[...]
    dself[...] = dot_full(ds_ref[...], dw_ref[...]) + db_ref[...]

    def forward_docs(h):
        def pass_on(k, _):
            r = mate_from(k) * 2 + c0
            got(dg.at[h, r], dg.at[h, r], s1.at[h, k], v1.at[h, k])
            send(dg.at[h, r], dg.at[h, r], s1c.at[h, k], v1c.at[h, k], sibling)
            return 0

        lax.fori_loop(1, NZ * NYH, pass_on, 0)

    def wait_docs(h):
        def one(k, _):
            r = mate_from(k) * 2 + 1 - c0
            got(dg.at[h, r], dg.at[h, r], s1c.at[h, k], v1c.at[h, k])
            return 0

        lax.fori_loop(0, NZ * NYH, one, 0)

    def multiply(h, x):
        for j in range(2):
            both = jnp.dot(lhs[...], at[2 * x + j], preferred_element_type=jnp.float32)
            whole = both[:128] + both[128:]
            part[h, 4 * x + 2 * j] = whole[:, :128]
            part[h, 4 * x + 2 * j + 1] = whole[:, 128:]

    xp, xm, xo = (x0 + 1) % NX, (x0 + NX - 1) % NX, (x0 + 2) % NX

    def start_x(h):
        docs = dg[h].reshape(DT * 128, 128).T
        high, low = split_two(docs)
        lhs[0:128, :] = high
        lhs[128:256, :] = low
        multiply(h, xo)
        send(part.at[h, pl.ds(4 * xo, 2)], r2.at[h, 0], sx1.at[h, 0], vx1.at[h, 0], x_dev(1))
        send(part.at[h, pl.ds(4 * xo + 2, 2)], r2.at[h, 1], sx1.at[h, 1], vx1.at[h, 1], x_dev(-1))
        multiply(h, xp)
        send(part.at[h, pl.ds(4 * xp + 2, 2)], rx.at[h, 0, 1], sx2.at[h, 0], vx2.at[h, 0], x_dev(1))
        multiply(h, xm)
        send(part.at[h, pl.ds(4 * xm, 2)], rx.at[h, 1, 0], sx2.at[h, 1], vx2.at[h, 1], x_dev(-1))
        multiply(h, x0)

    def second_x(h):
        got(r2.at[h, 0], r2.at[h, 0], sx1.at[h, 0], vx1.at[h, 0])
        part[h, pl.ds(4 * xp, 2)] += r2[h, 0]
        send(part.at[h, pl.ds(4 * xp, 2)], rx.at[h, 0, 0], sx2.at[h, 2], vx2.at[h, 2], x_dev(1))
        got(r2.at[h, 1], r2.at[h, 1], sx1.at[h, 1], vx1.at[h, 1])
        part[h, pl.ds(4 * xm + 2, 2)] += r2[h, 1]
        send(part.at[h, pl.ds(4 * xm + 2, 2)], rx.at[h, 1, 1], sx2.at[h, 3], vx2.at[h, 3], x_dev(-1))

    def start_y(h):
        for i, (a, b) in enumerate(((0, 1), (1, 0), (0, 0), (1, 1))):
            got(rx.at[h, a, b], rx.at[h, a, b], sx2.at[h, i], vx2.at[h, i])
        for b in range(2):
            sx[h, 2 * b : 2 * b + 2] = part[h, pl.ds(4 * x0 + 2 * b, 2)] + rx[h, 0, b] + rx[h, 1, b]
        for k in range(1, NYL):
            send(sx.at[h, (y0 + k) % NYL], ry.at[h, k - 1], sy.at[h, k - 1], vy.at[h, k - 1], y_dev(k))

    def end_y(h):
        for k in range(NYL - 1):
            got(ry.at[h, k], ry.at[h, k], sy.at[h, k], vy.at[h, k])
        return ((sx[h, y0] + ry[h, 0]) + (ry[h, 1] + ry[h, 2])) * qinv_row

    forward_docs(0)
    wait_docs(0)
    start_x(0)
    forward_docs(1)
    wait_docs(1)
    start_x(1)
    second_x(0)
    second_x(1)
    start_y(0)
    start_y(1)
    agg = jnp.concatenate([end_y(0).T, end_y(1).T], axis=1)

    query_out = rms(qself[...] + dot_full(agg, qnw_ref[...]))
    qo_ref[...] = query_out
    query_scaled = query_out * qinv
    for h in range(2):
        qg[h, col] = query_scaled[:, h * 128 : (h + 1) * 128]

    def share(h, block, sem, dev):
        send(qg.at[h, block], qg.at[h, block], s3.at[h, sem], v3.at[h, block], dev)

    def have(h, block):
        got(qg.at[h, block], qg.at[h, block], s3.at[h, 0], v3.at[h, block])

    def own_out(h):
        for k in range(1, NYL):
            share(h, col, k - 1, y_dev(k))
        share(h, col, 3, x_dev(1))
        share(h, col, 4, x_dev(-1))

    def y_on(h):
        for k in range(1, NYL):
            block = x0 * NYL + (y0 + NYL - k) % NYL
            have(h, block)
            share(h, block, 3 + 2 * k, x_dev(1))
            share(h, block, 4 + 2 * k, x_dev(-1))

    def x_on(h, k):
        y = (y0 + NYL - k) % NYL
        way = 1 - 2 * (y // 2)
        block = (x0 - way + NX) % NX * NYL + y
        have(h, block)
        share(h, block, 11 + k, x_dev(way))

    def x_rest(h):
        for k in range(NYL):
            y = (y0 + NYL - k) % NYL
            way = 1 - 2 * (y // 2)
            have(h, (x0 + way + NX) % NX * NYL + y)
        for y in range(NYL):
            have(h, xo * NYL + y)

    own_out(0)
    own_out(1)
    y_on(0)
    x_on(0, 0)
    y_on(1)
    for k in range(1, NYL):
        x_on(0, k)
    x_on(1, 0)
    x_rest(0)

    def back(h):
        for j in range(QT // 2):
            high, low = split_two(qg[h, 2 * j : 2 * j + 2].reshape(256, 128))
            wq[j, :, 0:128] = high
            wq[j, :, 128:256] = low

        def rows_of(i, _):
            total = jnp.zeros((256, 256), jnp.float32)
            for j in range(QT // 2):
                total += jnp.dot(at[j, pl.ds(i * 256, 256), :], wq[j], preferred_element_type=jnp.float32)
            whole = (total[:, :128] + total[:, 128:]).reshape(4, 2, 32, 128)
            yd[h, 0, pl.ds(i * 4, 4)] = whole[:, 0]
            yd[h, 1, pl.ds(i * 4, 4)] = whole[:, 1]
            return 0

        lax.fori_loop(0, 4, rows_of, 0)
        send(yd.at[h, 1 - c0], rc.at[h], s4c.at[h], v4c.at[h], sibling)

    def spread(h):
        got(rc.at[h], rc.at[h], s4c.at[h], v4c.at[h])
        zd[h] = yd[h, c0] + rc[h]

        def push(k, _):
            send(zd.at[h, mate(k)], rd.at[h, k], s4.at[h, k], v4.at[h, k], (mate(k) * 2 + c0, col))
            return 0

        lax.fori_loop(1, NZ * NYH, push, 0)

    def collect(h):
        def one(k, total):
            got(rd.at[h, k], rd.at[h, k], s4.at[h, k], v4.at[h, k])
            return total + rd[h, k]

        return lax.fori_loop(1, NZ * NYH, one, zd[h, m0])

    back(0)
    for k in range(1, NYL):
        x_on(1, k)
    spread(0)
    x_rest(1)
    back(1)
    spread(1)
    doc_agg = jnp.concatenate([collect(0), collect(1)], axis=1) * dinv
    do_ref[...] = rms(dself[...] + dot_full(doc_agg, dnw_ref[...]))

    for h in range(2):
        def out_docs(k, _, h=h):
            sent(dg.at[h, row], dg.at[h, row], s1.at[h, k], v1.at[h, k])
            sent(zd.at[h, 0], rd.at[h, k], s4.at[h, k], v4.at[h, k])
            return 0

        lax.fori_loop(1, NZ * NYH, out_docs, 0)

        def out_sibling(k, _, h=h):
            sent(dg.at[h, row], dg.at[h, row], s1c.at[h, k], v1c.at[h, k])
            return 0

        lax.fori_loop(0, NZ * NYH, out_sibling, 0)
        for i in range(2):
            sent(r2.at[h, i], r2.at[h, i], sx1.at[h, i], vx1.at[h, i])
        for i in range(4):
            sent(rx.at[h, 0, 0], rx.at[h, 0, 0], sx2.at[h, i], vx2.at[h, i])
        for k in range(NYL - 1):
            sent(ry.at[h, k], ry.at[h, k], sy.at[h, k], vy.at[h, k])

        def out_query(k, _, h=h):
            sent(qg.at[h, 0], qg.at[h, 0], s3.at[h, k], v3.at[h, 0])
            return 0

        lax.fori_loop(0, 15, out_query, 0)
        sent(rc.at[h], rc.at[h], s4c.at[h], v4c.at[h])


def local(
    query_state, doc_state, query_degree, doc_degree, tile_slots, tile_count, tile_bits,
    query_self_w, query_nbr_w, query_bias, doc_self_w, doc_nbr_w, doc_bias,
):
    f32, bf16 = jnp.float32, jnp.bfloat16
    smem = pl.BlockSpec(memory_space=pltpu.SMEM)
    dma = pltpu.SemaphoreType.DMA
    args = (
        query_state, doc_state, query_degree.reshape(1, 128), doc_degree.reshape(1, 32),
        tile_slots[0], tile_count, jnp.swapaxes(tile_bits[0, 0], 1, 2),
        query_self_w, query_nbr_w, query_bias.reshape(1, 256),
        doc_self_w, doc_nbr_w, doc_bias.reshape(1, 256),
    )

    def whole(a):
        return pl.BlockSpec(a.shape, lambda i: (0,) * len(a.shape))

    return pl.pallas_call(
        kernel,
        out_shape=(
            jax.ShapeDtypeStruct((128, 256), f32),
            jax.ShapeDtypeStruct((32, 256), f32),
        ),
        grid=(1,),
        in_specs=[smem if i in (4, 5) else whole(a) for i, a in enumerate(args)],
        out_specs=(whole(query_state), whole(doc_state)),
        scratch_shapes=[
            pltpu.VMEM((QT // 2, DT * 128, 256), bf16),
            pltpu.VMEM((2, 32, 32, 128), f32),
            pltpu.VMEM((256, DT * 128), bf16),
            pltpu.VMEM((2, QT, 128, 128), f32),
            pltpu.VMEM((2, 2, 2, 128, 128), f32),
            pltpu.VMEM((2, 2, 2, 2, 128, 128), f32),
            pltpu.VMEM((2, NYL, 128, 128), f32),
            pltpu.VMEM((2, NYL - 1, 128, 128), f32),
            pltpu.VMEM((2, QT, 128, 128), f32),
            pltpu.VMEM((QT // 2, 256, 256), bf16),
            pltpu.VMEM((2, 2, 16, 32, 128), f32),
            pltpu.VMEM((2, 16, 32, 128), f32),
            pltpu.VMEM((2, 16, 32, 128), f32),
            pltpu.VMEM((2, 16, 32, 128), f32),
            pltpu.VMEM((128, 256), f32),
            pltpu.VMEM((32, 256), f32),
            dma((2, 16)), dma((2, 16)), dma((2, 16)), dma((2, 16)),
            dma((2, 2)), dma((2, 2)), dma((2, 4)), dma((2, 4)),
            dma((2, 3)), dma((2, 3)), dma((2, 15)), dma((2, 16)),
            dma((2,)), dma((2,)), dma((2, 16)), dma((2, 16)),
        ],
        compiler_params=pltpu.CompilerParams(
            collective_id=0, has_side_effects=True, vmem_limit_bytes=56 << 20
        ),
    )(*args)


def solution(mesh):
    placed = (
        P(("row", "col"), None),
        P(("col", "row"), None),
        P(("row", "col")),
        P(("col", "row")),
        P("row", "col", None),
        P("row", "col"),
        P("row", "col", None, None, None),
        P(),
        P(),
        P(),
        P(),
        P(),
        P(),
    )
    return jax.shard_map(
        local,
        mesh=mesh,
        in_specs=placed,
        out_specs=(P(("row", "col"), None), P(("col", "row"), None)),
        check_vma=False,
    )
```

```python
import functools

import jax
import jax.numpy as jnp
from jax import lax
from jax.experimental import pallas as pl
from jax.experimental.pallas import tpu as pltpu
from jax.sharding import PartitionSpec as P

QT = 16
DT = 8
TMAX = 96
NX, NYL, NZ, NYH = 4, 4, 8, 2
Y_ORDER = (3, 2, 1)
MESH = pl.DeviceIdType.MESH
HIGHEST = lax.Precision.HIGHEST


def split_two(x):
    high = x.astype(jnp.bfloat16)
    low = (x - high.astype(jnp.float32)).astype(jnp.bfloat16)
    return high, low


def column_of(row_vector):
    n = row_vector.shape[1]
    i = lax.broadcasted_iota(jnp.int32, (n, n), 0)
    j = lax.broadcasted_iota(jnp.int32, (n, n), 1)
    return jnp.sum(jnp.where(i == j, row_vector, 0.0), axis=1, keepdims=True)


def rms(before):
    hidden = jnp.maximum(before, 0.0)
    return hidden * lax.rsqrt(jnp.mean(hidden * hidden, axis=-1, keepdims=True) + 1e-05)


def dot_full(a, b):
    return jnp.dot(a, b, precision=HIGHEST, preferred_element_type=jnp.float32)


def kernel(
    qs_ref, ds_ref, qdeg_ref, ddeg_ref, slots_ref, count_ref, bits_ref,
    qw_ref, qnw_ref, qb_ref, dw_ref, dnw_ref, db_ref,
    qo_ref, do_ref,
    at, dg, lhs, part, r2, rx, sx, ry, qg, wq, yd, rc, zd, rd, qself, dself,
    s1, v1, s1c, v1c, sx1, vx1, sx2, vx2, sy, vy, s3, v3, s4c, v4c, s4, v4,
):
    row = lax.axis_index("row")
    col = lax.axis_index("col")
    z0, h0, c0 = row // 4, (row // 2) % 2, row % 2
    x0, y0 = col // NYL, col % NYL
    m0 = z0 * 2 + h0
    sibling = (row + 1 - 2 * c0, col)

    def mate(k):
        dz, dh = k // 2, k % 2
        return (z0 + dz) % NZ * 2 + (h0 + dh) % 2

    def mate_from(k):
        dz, dh = k // 2, k % 2
        return (z0 + NZ - dz) % NZ * 2 + (h0 + dh) % 2

    def x_dev(dx):
        return (row, (x0 + dx + NX) % NX * NYL + y0)

    def y_dev(k):
        return (row, x0 * NYL + (y0 + k) % NYL)

    def send(src, dst, ssem, rsem, dev):
        copy = pltpu.make_async_remote_copy(
            src_ref=src, dst_ref=dst, send_sem=ssem, recv_sem=rsem, device_id=dev, device_id_type=MESH
        )
        copy.start()
        return copy

    def sent(src, dst, ssem, rsem):
        pltpu.make_async_remote_copy(
            src_ref=src, dst_ref=dst, send_sem=ssem, recv_sem=rsem, device_id=sibling, device_id_type=MESH
        ).wait_send()

    def got(src, dst, ssem, rsem):
        pltpu.make_async_remote_copy(
            src_ref=src, dst_ref=dst, send_sem=ssem, recv_sem=rsem, device_id=sibling, device_id_type=MESH
        ).wait_recv()

    barrier = pltpu.get_barrier_semaphore()

    def greet(dev):
        pl.semaphore_signal(barrier, inc=1, device_id=dev, device_id_type=MESH)

    greet(sibling)
    greet(x_dev(1))
    greet(x_dev(-1))
    for k in range(1, NYL):
        greet(y_dev(k))

    def greet_mate(k, _):
        greet((mate(k) * 2 + c0, col))
        return 0

    lax.fori_loop(1, NZ * NYH, greet_mate, 0)

    dinv = column_of(lax.rsqrt(ddeg_ref[...].astype(jnp.float32)))
    qinv_row = lax.rsqrt(qdeg_ref[...].astype(jnp.float32))
    qinv = column_of(qinv_row)
    scaled = ds_ref[...] * dinv
    for h in range(2):
        dg[h, row] = scaled[:, h * 128 : (h + 1) * 128]

    pl.semaphore_wait(barrier, 1 + 2 + NYL - 1 + NZ * NYH - 1)

    for h in range(2):
        send(dg.at[h, row], dg.at[h, row], s1c.at[h, 0], v1c.at[h, 0], sibling)

        def push(k, _, h=h):
            send(dg.at[h, row], dg.at[h, row], s1.at[h, k], v1.at[h, k], (mate(k) * 2 + c0, col))
            return 0

        lax.fori_loop(1, NZ * NYH, push, 0)

    shifts = lax.broadcasted_iota(jnp.int32, (8, 128), 0)
    count = count_ref[0, 0]

    def unpack(s, t):
        t_in = jnp.minimum(t, TMAX - 1)
        hit = jnp.logical_and(t < count, slots_ref[0, t_in] == s)
        keep = jnp.where(hit, 1, 0)
        words = bits_ref[t_in] * keep
        rows = []
        for w in range(16):
            spread = jnp.broadcast_to(words[w : w + 1, :], (8, 128))
            rows.append(jnp.bitwise_and(jnp.right_shift(spread, shifts), 1).astype(jnp.float32))
        tile = jnp.concatenate(rows, axis=0).astype(jnp.bfloat16)
        return tile, t + keep

    def unpack_pair(p, t):
        for half in range(2):
            for d in range(DT):
                tile, t = unpack((2 * p + half) * DT + d, t)
                at[p, d * 128 : (d + 1) * 128, half * 128 : (half + 1) * 128] = tile
        return t

    lax.fori_loop(0, QT // 2, unpack_pair, jnp.int32(0))

    qself[...] = dot_full(qs_ref[...], qw_ref[...]) + qb_ref[...]
    dself[...] = dot_full(ds_ref[...], dw_ref[...]) + db_ref[...]

    def forward_docs(h):
        def pass_on(k, _):
            r = mate_from(k) * 2 + c0
            got(dg.at[h, r], dg.at[h, r], s1.at[h, k], v1.at[h, k])
            send(dg.at[h, r], dg.at[h, r], s1c.at[h, k], v1c.at[h, k], sibling)
            return 0

        lax.fori_loop(1, NZ * NYH, pass_on, 0)

    def wait_docs(h):
        def one(k, _):
            r = mate_from(k) * 2 + 1 - c0
            got(dg.at[h, r], dg.at[h, r], s1c.at[h, k], v1c.at[h, k])
            return 0

        lax.fori_loop(0, NZ * NYH, one, 0)

    def multiply(h, x):
        for j in range(2):
            both = jnp.dot(lhs[...], at[2 * x + j], preferred_element_type=jnp.float32)
            whole = both[:128] + both[128:]
            part[h, 4 * x + 2 * j] = whole[:, :128]
            part[h, 4 * x + 2 * j + 1] = whole[:, 128:]

    xp, xm, xo = (x0 + 1) % NX, (x0 + NX - 1) % NX, (x0 + 2) % NX

    def start_x(h):
        docs = dg[h].reshape(DT * 128, 128).T
        high, low = split_two(docs)
        lhs[0:128, :] = high
        lhs[128:256, :] = low
        multiply(h, xo)
        send(part.at[h, pl.ds(4 * xo, 2)], r2.at[h, 0], sx1.at[h, 0], vx1.at[h, 0], x_dev(1))
        send(part.at[h, pl.ds(4 * xo + 2, 2)], r2.at[h, 1], sx1.at[h, 1], vx1.at[h, 1], x_dev(-1))
        multiply(h, xp)
        send(part.at[h, pl.ds(4 * xp + 2, 2)], rx.at[h, 0, 1], sx2.at[h, 0], vx2.at[h, 0], x_dev(1))
        multiply(h, xm)
        send(part.at[h, pl.ds(4 * xm, 2)], rx.at[h, 1, 0], sx2.at[h, 1], vx2.at[h, 1], x_dev(-1))
        multiply(h, x0)

    def second_x(h):
        got(r2.at[h, 0], r2.at[h, 0], sx1.at[h, 0], vx1.at[h, 0])
        part[h, pl.ds(4 * xp, 2)] += r2[h, 0]
        send(part.at[h, pl.ds(4 * xp, 2)], rx.at[h, 0, 0], sx2.at[h, 2], vx2.at[h, 2], x_dev(1))
        got(r2.at[h, 1], r2.at[h, 1], sx1.at[h, 1], vx1.at[h, 1])
        part[h, pl.ds(4 * xm + 2, 2)] += r2[h, 1]
        send(part.at[h, pl.ds(4 * xm + 2, 2)], rx.at[h, 1, 1], sx2.at[h, 3], vx2.at[h, 3], x_dev(-1))

    def start_y(h):
        for i, (a, b) in enumerate(((0, 1), (1, 0), (0, 0), (1, 1))):
            got(rx.at[h, a, b], rx.at[h, a, b], sx2.at[h, i], vx2.at[h, i])
        for b in range(2):
            sx[h, 2 * b : 2 * b + 2] = part[h, pl.ds(4 * x0 + 2 * b, 2)] + rx[h, 0, b] + rx[h, 1, b]
        for k in Y_ORDER:
            send(sx.at[h, (y0 + k) % NYL], ry.at[h, k - 1], sy.at[h, k - 1], vy.at[h, k - 1], y_dev(k))

    def end_y(h):
        for k in range(NYL - 1):
            got(ry.at[h, k], ry.at[h, k], sy.at[h, k], vy.at[h, k])
        return ((sx[h, y0] + ry[h, 0]) + (ry[h, 1] + ry[h, 2])) * qinv_row

    forward_docs(0)
    wait_docs(0)
    start_x(0)
    forward_docs(1)
    wait_docs(1)
    start_x(1)
    second_x(0)
    second_x(1)
    start_y(0)
    start_y(1)
    agg = jnp.concatenate([end_y(0).T, end_y(1).T], axis=1)

    query_out = rms(qself[...] + dot_full(agg, qnw_ref[...]))
    qo_ref[...] = query_out
    query_scaled = query_out * qinv
    for h in range(2):
        qg[h, col] = query_scaled[:, h * 128 : (h + 1) * 128]

    def share(h, block, sem, dev):
        send(qg.at[h, block], qg.at[h, block], s3.at[h, sem], v3.at[h, block], dev)

    def have(h, block):
        got(qg.at[h, block], qg.at[h, block], s3.at[h, 0], v3.at[h, block])

    def own_out(h):
        for k in Y_ORDER:
            share(h, col, k - 1, y_dev(k))
        share(h, col, 3, x_dev(1))
        share(h, col, 4, x_dev(-1))

    def y_on(h):
        for k in Y_ORDER:
            block = x0 * NYL + (y0 + NYL - k) % NYL
            have(h, block)
            share(h, block, 3 + 2 * k, x_dev(1))
            share(h, block, 4 + 2 * k, x_dev(-1))

    def x_on(h, k):
        y = (y0 + NYL - k) % NYL
        way = 1 - 2 * (y // 2)
        block = (x0 - way + NX) % NX * NYL + y
        have(h, block)
        share(h, block, 11 + k, x_dev(way))

    def x_rest(h):
        for k in range(NYL):
            y = (y0 + NYL - k) % NYL
            way = 1 - 2 * (y // 2)
            have(h, (x0 + way + NX) % NX * NYL + y)
        for y in range(NYL):
            have(h, xo * NYL + y)

    own_out(0)
    own_out(1)
    y_on(0)
    x_on(0, 0)
    y_on(1)
    for k in Y_ORDER:
        x_on(0, k)
    x_on(1, 0)
    for k in Y_ORDER:
        x_on(1, k)
    x_rest(0)

    def back(h):
        for j in range(QT // 2):
            high, low = split_two(qg[h, 2 * j : 2 * j + 2].reshape(256, 128))
            wq[j, :, 0:128] = high
            wq[j, :, 128:256] = low

        def rows_of(i, _):
            total = jnp.zeros((256, 256), jnp.float32)
            for j in range(QT // 2):
                total += jnp.dot(at[j, pl.ds(i * 256, 256), :], wq[j], preferred_element_type=jnp.float32)
            whole = (total[:, :128] + total[:, 128:]).reshape(4, 2, 32, 128)
            yd[h, 0, pl.ds(i * 4, 4)] = whole[:, 0]
            yd[h, 1, pl.ds(i * 4, 4)] = whole[:, 1]
            return 0

        lax.fori_loop(0, 4, rows_of, 0)
        send(yd.at[h, 1 - c0], rc.at[h], s4c.at[h], v4c.at[h], sibling)

    def spread(h):
        got(rc.at[h], rc.at[h], s4c.at[h], v4c.at[h])
        zd[h] = yd[h, c0] + rc[h]

        def push(k, _):
            send(zd.at[h, mate(k)], rd.at[h, k], s4.at[h, k], v4.at[h, k], (mate(k) * 2 + c0, col))
            return 0

        lax.fori_loop(1, NZ * NYH, push, 0)

    def collect(h):
        def one(k, total):
            got(rd.at[h, k], rd.at[h, k], s4.at[h, k], v4.at[h, k])
            return total + rd[h, k]

        return lax.fori_loop(1, NZ * NYH, one, zd[h, m0])

    back(0)
    spread(0)
    x_rest(1)
    back(1)
    spread(1)
    doc_agg = jnp.concatenate([collect(0), collect(1)], axis=1) * dinv
    do_ref[...] = rms(dself[...] + dot_full(doc_agg, dnw_ref[...]))

    for h in range(2):
        def out_docs(k, _, h=h):
            sent(dg.at[h, row], dg.at[h, row], s1.at[h, k], v1.at[h, k])
            sent(zd.at[h, 0], rd.at[h, k], s4.at[h, k], v4.at[h, k])
            return 0

        lax.fori_loop(1, NZ * NYH, out_docs, 0)

        def out_sibling(k, _, h=h):
            sent(dg.at[h, row], dg.at[h, row], s1c.at[h, k], v1c.at[h, k])
            return 0

        lax.fori_loop(0, NZ * NYH, out_sibling, 0)
        for i in range(2):
            sent(r2.at[h, i], r2.at[h, i], sx1.at[h, i], vx1.at[h, i])
        for i in range(4):
            sent(rx.at[h, 0, 0], rx.at[h, 0, 0], sx2.at[h, i], vx2.at[h, i])
        for k in range(NYL - 1):
            sent(ry.at[h, k], ry.at[h, k], sy.at[h, k], vy.at[h, k])

        def out_query(k, _, h=h):
            sent(qg.at[h, 0], qg.at[h, 0], s3.at[h, k], v3.at[h, 0])
            return 0

        lax.fori_loop(0, 15, out_query, 0)
        sent(rc.at[h], rc.at[h], s4c.at[h], v4c.at[h])


def local(
    query_state, doc_state, query_degree, doc_degree, tile_slots, tile_count, tile_bits,
    query_self_w, query_nbr_w, query_bias, doc_self_w, doc_nbr_w, doc_bias,
):
    f32, bf16 = jnp.float32, jnp.bfloat16
    smem = pl.BlockSpec(memory_space=pltpu.SMEM)
    dma = pltpu.SemaphoreType.DMA
    args = (
        query_state, doc_state, query_degree.reshape(1, 128), doc_degree.reshape(1, 32),
        tile_slots[0], tile_count, jnp.swapaxes(tile_bits[0, 0], 1, 2),
        query_self_w, query_nbr_w, query_bias.reshape(1, 256),
        doc_self_w, doc_nbr_w, doc_bias.reshape(1, 256),
    )

    def whole(a):
        return pl.BlockSpec(a.shape, lambda i: (0,) * len(a.shape))

    return pl.pallas_call(
        kernel,
        out_shape=(
            jax.ShapeDtypeStruct((128, 256), f32),
            jax.ShapeDtypeStruct((32, 256), f32),
        ),
        grid=(1,),
        in_specs=[smem if i in (4, 5) else whole(a) for i, a in enumerate(args)],
        out_specs=(whole(query_state), whole(doc_state)),
        scratch_shapes=[
            pltpu.VMEM((QT // 2, DT * 128, 256), bf16),
            pltpu.VMEM((2, 32, 32, 128), f32),
            pltpu.VMEM((256, DT * 128), bf16),
            pltpu.VMEM((2, QT, 128, 128), f32),
            pltpu.VMEM((2, 2, 2, 128, 128), f32),
            pltpu.VMEM((2, 2, 2, 2, 128, 128), f32),
            pltpu.VMEM((2, NYL, 128, 128), f32),
            pltpu.VMEM((2, NYL - 1, 128, 128), f32),
            pltpu.VMEM((2, QT, 128, 128), f32),
            pltpu.VMEM((QT // 2, 256, 256), bf16),
            pltpu.VMEM((2, 2, 16, 32, 128), f32),
            pltpu.VMEM((2, 16, 32, 128), f32),
            pltpu.VMEM((2, 16, 32, 128), f32),
            pltpu.VMEM((2, 16, 32, 128), f32),
            pltpu.VMEM((128, 256), f32),
            pltpu.VMEM((32, 256), f32),
            dma((2, 16)), dma((2, 16)), dma((2, 16)), dma((2, 16)),
            dma((2, 2)), dma((2, 2)), dma((2, 4)), dma((2, 4)),
            dma((2, 3)), dma((2, 3)), dma((2, 15)), dma((2, 16)),
            dma((2,)), dma((2,)), dma((2, 16)), dma((2, 16)),
        ],
        compiler_params=pltpu.CompilerParams(
            collective_id=0, has_side_effects=True, vmem_limit_bytes=56 << 20
        ),
    )(*args)


def solution(mesh):
    placed = (
        P(("row", "col"), None),
        P(("col", "row"), None),
        P(("row", "col")),
        P(("col", "row")),
        P("row", "col", None),
        P("row", "col"),
        P("row", "col", None, None, None),
        P(),
        P(),
        P(),
        P(),
        P(),
        P(),
    )
    return jax.shard_map(
        local,
        mesh=mesh,
        in_specs=placed,
        out_specs=(P(("row", "col"), None), P(("col", "row"), None)),
        check_vma=False,
    )
```
